512 devices in a mesh: grp: 16 (over y_lo, z), blk: 32 (over x, y_hi, core).
Axes of the slice: x: 4, y: 8 (y_hi: 4, y_lo: 2; y = y_hi * 2 + y_lo), z: 8, core: 2. Of those that a mesh axis runs over, the one named last changes fastest.
Arguments:
- modes: bfloat16 [3, 256, 32, 128, 128], P(None, None, 'grp', 'blk'), may hold values from -6 to 6
- metric: float32 [3, 32, 128, 128], P(None, 'grp', 'blk'), may hold values from 0.5 to 2
- block_map: int32 [32, 128, 128], P('grp', 'blk'), may hold values from 0 to 15
- flags: int32 [32, 128, 128], P('grp', 'blk'), may hold values from 0 to 2
- region_scale: float32 [16], replicated, may hold values from 0.5 to 2
Outputs:
- tensor: float32 [8, 256, 256], P(None, 'grp', 'blk')
The draws below stay inside these ranges and needn't reach their ends.
All inputs are finite; a program needn't handle non-finite values.
Results may differ from the reference program's by a relative error of at most 0.0042.
Values may be sent and summed in bfloat16 or wider, within the bound.
A program may use at most 64 MiB of HBM per device.

```python
import math
import jax
import jax.numpy as jnp
from jax import lax

M = 256
KS = 8
REGIONS = 16
NZ = 128
NX = 32
NY = 128


def set_ends(entries, rng, smallest, high):
    spot = [jax.random.randint(jax.random.fold_in(rng, axis), (), 0, length) for axis, length in enumerate(entries.shape)]
    main_axis = entries.shape.index(max(entries.shape))
    neighbour = spot[:main_axis] + [(spot[main_axis] + 1) % entries.shape[main_axis]] + spot[main_axis + 1:]
    return entries.at[tuple(spot)].set(smallest).at[tuple(neighbour)].set(high)


def levels(stream_key, dims, pieces, smallest, high):
    def one(dim, shards_of):
        steps = jax.random.uniform(jax.random.fold_in(jax.random.fold_in(stream_key, 6), dim), (shards_of,), jnp.float32, smallest / len(pieces), high / len(pieces))
        return jnp.repeat(jnp.exp(steps), dims[dim] // shards_of).reshape((-1,) + (1,) * (len(dims) - dim - 1))

    gain = one(*pieces[0])
    for cut in pieces[1:]:
        gain = gain * one(*cut)
    return gain


def normal_values(rng, extent, deviation, reach, pieces=(), kind=jnp.bfloat16):
    level = levels(rng, extent, pieces, -0.22, 0.18) if pieces else 1.0
    drawn = jax.random.normal(rng, extent, jnp.float32) * deviation * level
    return jnp.minimum(jnp.maximum(drawn, -reach), reach).astype(kind)


def setup_inputs(seed: int = 0) -> dict:
    key_list = jax.random.split(jax.random.key(seed), 6)
    return {
        "modes": normal_values(key_list[0], (3, M, NX, NY, NZ), 1.0, 6.0, ((2, 16), (3, 32))),
        "metric": jnp.clip(jnp.exp(math.log(2.0) - 1.3862944 * jax.random.uniform(key_list[1], (3, NX, NY, NZ), jnp.float32) ** levels(key_list[1], (3, NX, NY, NZ), ((1, 16), (2, 32)), -0.2, 0.2)), 0.5, 2.0),
        "block_map": set_ends(jax.random.randint(key_list[2], (NX, NY, NZ), 0, REGIONS), jax.random.fold_in(key_list[2], 1), 0, REGIONS - 1).astype(jnp.int32),
        "flags": set_ends(jax.random.randint(key_list[3], (NX, NY, NZ), 0, 3), jax.random.fold_in(key_list[3], 1), 0, 2).astype(jnp.int32),
        "region_scale": jnp.clip(jnp.exp(jax.random.uniform(key_list[4], (REGIONS,), jnp.float32, math.log(0.5), math.log(2.0))), 0.5, 2.0),
    }


def stencil(padded, metric):
    gx = 0.5 * (padded[:, :, 2:, 1:-1, 1:-1] - padded[:, :, :-2, 1:-1, 1:-1]) * metric[0]
    gy = 0.5 * (padded[:, :, 1:-1, 2:, 1:-1] - padded[:, :, 1:-1, :-2, 1:-1]) * metric[1]
    gz = 0.5 * (padded[:, :, 1:-1, 1:-1, 2:] - padded[:, :, 1:-1, 1:-1, :-2]) * metric[2]
    return jnp.stack([gx, gy, gz])


def weights(block_map, flags, region_scale, metric, norm):
    labels = jnp.arange(region_scale.shape[0], dtype=jnp.int32)[:, None, None, None]
    scale = jnp.sum(jnp.where(block_map[None] == labels, region_scale[:, None, None, None], jnp.float32(0.0)), axis=0)
    fluid = jnp.where(flags == 0, jnp.float32(1.0), jnp.where(flags == 1, jnp.float32(0.0), jnp.float32(0.5)))
    return scale * fluid * norm / (metric[0] * metric[1] * metric[2])


def reference(modes, metric, block_map, flags, region_scale):
    norm = float(NX * NY * NZ) ** -0.5
    slab = modes[:, :KS].astype(jnp.float32)
    padded = jnp.pad(slab, ((0, 0), (0, 0), (1, 1), (1, 1), (1, 1)))
    grads = stencil(padded, metric)
    weight = weights(block_map, flags, region_scale, metric, norm)
    results = []
    for k in range(KS):
        grad_k = grads[:, :, k]

        def row(xi, total):
            local = lax.dynamic_slice_in_dim(modes, xi, 1, 2).astype(jnp.float32)
            grad_row = lax.dynamic_slice_in_dim(grad_k, xi, 1, 2)
            weight_row = lax.dynamic_slice_in_dim(weight, xi, 1, 0)
            mixed = local[0][None] * grad_row[:, 0][:, None]
            mixed = mixed + local[1][None] * grad_row[:, 1][:, None]
            mixed = mixed + local[2][None] * grad_row[:, 2][:, None]
            tested = (weight_row[None, None] * mixed).astype(jnp.bfloat16)
            tested = lax.optimization_barrier(tested).astype(jnp.float32)
            return total + lax.dot_general(tested, local, (((0, 2, 3, 4), (0, 2, 3, 4)), ((), ())), precision=lax.Precision.HIGHEST)

        total = lax.fori_loop(0, NX, row, jnp.zeros((M, M), jnp.float32))
        results.append(total)
    return jnp.stack(results)
```

```python
import functools

import jax
import jax.numpy as jnp
from jax import lax
from jax.experimental import pallas as pl
from jax.experimental.pallas import tpu as pltpu
from jax.sharding import PartitionSpec as P

KS = 8
M = 256
CELLS = 8
NX, NY = 2, 4
F32, BF16 = jnp.float32, jnp.bfloat16
MESH = pl.DeviceIdType.MESH
BLOCKS = 4


def kernel(
    norm,
    modes_hbm, metric_hbm, map_hbm, flags_hbm, scale_ref,
    out_ref,
    nat, natf, slab, slabf, met, bmap, flg, gtab, bmat, pacc,
    hx_send, hy_send, hx_recv, hy_recv,
    c_send, c_recv, x_send, x_recv, y_send, y_recv, z_send, z_recv, own,
    in_sem, h_ssem, h_rsem, c_ssem, c_rsem, x_ssem, x_rsem, y_ssem, y_rsem, z_ssem, z_rsem,
):
    grp = lax.axis_index("grp")
    blk = lax.axis_index("blk")
    z, y_lo = grp % 8, grp // 8
    core, y_hi, x = blk % 2, (blk // 2) % 4, blk // 8

    def at(dx=0, dyh=0, dyl=0, dz=0, dc=0):
        g = ((y_lo + dyl) % 2) * 8 + (z + dz) % 8
        b = ((x + dx) % 4) * 8 + ((y_hi + dyh) % 4) * 2 + (core + dc) % 2
        return (g, b)

    halo_to = [
        ((grp + 1) % 16, blk),
        ((grp + 15) % 16, blk),
        (grp, (blk + 1) % 32),
        (grp, (blk + 31) % 32),
    ]
    yrel = [(s, t) for s in range(4) for t in range(2)]
    partners = list(halo_to)
    partners.append(at(dc=1))
    partners += [at(dx=r) for r in range(1, 4)]
    partners += [at(dyh=s, dyl=t) for s, t in yrel[1:]]
    partners += [at(dz=q) for q in range(1, 8)]

    barrier = pltpu.get_barrier_semaphore()
    for p in partners:
        pl.semaphore_signal(barrier, inc=1, device_id=p, device_id_type=MESH)

    loads = [
        pltpu.make_async_copy(modes_hbm.at[:, pl.ds(0, KS * CELLS), :], slab, in_sem.at[0]),
        pltpu.make_async_copy(metric_hbm, met, in_sem.at[1]),
        pltpu.make_async_copy(map_hbm, bmap, in_sem.at[2]),
        pltpu.make_async_copy(flags_hbm, flg, in_sem.at[3]),
        pltpu.make_async_copy(modes_hbm, nat, in_sem.at[4]),
    ]
    for c in loads:
        c.start()

    loads[0].wait()
    for c in range(3):
        slabf[c * 64:(c + 1) * 64, :] = slab[c].astype(F32)

    def tile(c, row):
        return slabf[pl.ds(c * 64 + row, KS, stride=CELLS), :]

    s = {(c, row): tile(c, row) for c in range(3) for row in range(CELLS)}
    for side, xi in ((0, 1), (1, 0)):
        for c in range(3):
            for yp in range(2):
                a = s[c, xi * NY + 2 * yp]
                b = s[c, xi * NY + 2 * yp + 1]
                at_row = (c * 2 + yp) * 16
                hx_send[side, at_row:at_row + 16, :] = jnp.concatenate([a, b], 0).astype(BF16)
    for side, yi in ((0, 3), (1, 0)):
        for c in range(3):
            a, b = s[c, yi], s[c, NY + yi]
            hy_send[side, c * 16:c * 16 + 16, :] = jnp.concatenate([a, b], 0).astype(BF16)

    pl.semaphore_wait(barrier, len(partners))

    def remote(src, dst, ssem, rsem, to):
        return pltpu.make_async_remote_copy(
            src_ref=src, dst_ref=dst, send_sem=ssem, recv_sem=rsem,
            device_id=to, device_id_type=MESH,
        )

    halo = []
    for n in range(4):
        src, dst = (hx_send, hx_recv) if n < 2 else (hy_send, hy_recv)
        halo.append(remote(src.at[n % 2], dst.at[n % 2], h_ssem.at[n], h_rsem.at[n], halo_to[n]))
        halo[-1].start()

    loads[1].wait()
    loads[2].wait()
    loads[3].wait()
    region = bmap[...]
    scale = jnp.zeros((CELLS, 128), F32)
    for r in range(16):
        scale = jnp.where(region == r, scale_ref[r], scale)
    kinds = flg[...]
    fluid = jnp.where(kinds == 0, F32(1.0), jnp.where(kinds == 1, F32(0.0), F32(0.5)))
    m = [met[d * CELLS:(d + 1) * CELLS, :] for d in range(3)]
    weight = scale * fluid * norm / (m[0] * m[1] * m[2])
    half = [0.5 * weight * m[d] for d in range(3)]

    loads[4].wait()

    def widen(n, _):
        rows = pl.ds(pl.multiple_of(n * 256, 256), 256)
        for c in range(3):
            natf[c, rows, :] = nat[c, rows, :].astype(F32)
        return 0

    lax.fori_loop(0, 8, widen, 0)

    def spread(n, _):
        cc = (core + n // 4) % 2
        xx = (x + n % 4) % 4
        for pair in range(2):
            starts = []
            for e in range(2):
                yy = (y_hi + 2 * pair + e) % 4
                starts.append((xx * 8 + yy * 2 + cc) * (8 * CELLS))
            rows = pl.ds(pl.multiple_of(n * 32 + pair * 16, 16), 16)
            for d in range(3):
                for row in range(CELLS):
                    both = jnp.concatenate(
                        [natf[d, pl.ds(st + row, 8, stride=CELLS), :] for st in starts], 0
                    )
                    col = (row // 2) * 768 + d * 256 + (row % 2) * 128
                    bmat[rows, col:col + 128] = both.astype(BF16)
        return 0

    lax.fori_loop(0, 8, spread, 0)

    lane = lax.broadcasted_iota(jnp.int32, (KS, 128), 1)

    def put(d, c, row, diff):
        base = (d * 3 + c) * KS
        gtab[row, base:base + KS, :] = diff * half[d][row:row + 1, :]

    for c in range(3):
        for row in range(CELLS):
            v = s[c, row]
            after = jnp.where(lane == 127, F32(0.0), pltpu.roll(v, 127, 1))
            before = jnp.where(lane == 0, F32(0.0), pltpu.roll(v, 1, 1))
            put(2, c, row, after - before)

    for h in halo:
        h.wait_recv()
    keep = [
        jnp.where(grp > 0, F32(1.0), F32(0.0)),
        jnp.where(grp < 15, F32(1.0), F32(0.0)),
        jnp.where(blk > 0, F32(1.0), F32(0.0)),
        jnp.where(blk < 31, F32(1.0), F32(0.0)),
    ]
    for c in range(3):
        xs = [[None] * NY, [None] * NY]
        for side in range(2):
            for yp in range(2):
                at_row = (c * 2 + yp) * 16
                both = hx_recv[side, at_row:at_row + 16, :].astype(F32) * keep[side]
                xs[side][2 * yp], xs[side][2 * yp + 1] = both[:8], both[8:]
        ys = []
        for side in range(2):
            both = hy_recv[side, c * 16:c * 16 + 16, :].astype(F32) * keep[2 + side]
            ys.append((both[:8], both[8:]))
        for xi in range(NX):
            for yi in range(NY):
                row = xi * NY + yi
                hi = s[c, row + NY] if xi == 0 else xs[1][yi]
                lo = s[c, row - NY] if xi == 1 else xs[0][yi]
                put(0, c, row, hi - lo)
                hi = s[c, row + 1] if yi < NY - 1 else ys[1][xi]
                lo = s[c, row - 1] if yi > 0 else ys[0][xi]
                put(1, c, row, hi - lo)

    def compute(b):
        bases = []
        for t in range(2):
            for e in range(2):
                g = ((y_lo + t) % 2) * 8 + (z + 2 * b + e) % 8
                bases.append(g * (16 * CELLS))

        def rows_of(pair, d):
            halves = []
            for e in range(2):
                row = pair * 2 + e
                a = [
                    [natf[c, pl.ds(st + row, 16, stride=CELLS), :] for st in bases]
                    for c in range(3)
                ]
                a = [jnp.concatenate(v, 0) for v in a]
                per_k = []
                for k in range(KS):
                    g = [gtab[row, pl.ds((d * 3 + c) * KS + k, 1), :] for c in range(3)]
                    per_k.append((a[0] * g[0] + a[1] * g[1] + a[2] * g[2]).astype(BF16))
                halves.append(
                    jnp.concatenate(
                        [per_k[k][p * 16:p * 16 + 16] for p in range(4) for k in range(KS)], 0
                    )
                )
            return jnp.concatenate(halves, 1)

        def step(pair, _):
            total = None
            for d in range(3):
                tested = rows_of(pair, d)
                cols = pl.ds(pl.multiple_of(pair * 768 + d * 256, 256), 256)
                part = lax.dot_general(
                    bmat[:, cols], tested, (((1,), (1,)), ((), ())),
                    preferred_element_type=F32,
                )
                total = part if total is None else total + part
            pacc[b] = total + pacc[b]
            return 0

        pacc[b] = jnp.zeros((M, 512), F32)
        lax.fori_loop(0, 4, step, 0)

    sent = []

    def send(*args):
        c = remote(*args)
        c.start()
        sent.append(c)

    def send_core(b):
        c_send[b] = pacc[b, 128:256, :].astype(BF16)
        send(c_send.at[b], c_recv.at[b], c_ssem.at[b], c_rsem.at[b], at(dc=1))

    def arrived(dst, sem):
        pltpu.make_async_copy(dst, dst, sem).wait()

    def send_x(b):
        arrived(c_recv.at[b], c_rsem.at[b])
        for r in (2, 1, 3, 0):
            rows = slice(r * 32, r * 32 + 32)
            v = pacc[b, rows, :] + c_recv[b, rows, :].astype(F32)
            if r == 0:
                pacc[b, rows, :] = v
            else:
                x_send[b, r] = v.astype(BF16)
                send(x_send.at[b, r], x_recv.at[b, r], x_ssem.at[b, r], x_rsem.at[b, r], at(dx=r))

    def send_y(b):
        v = pacc[b, 0:32, :]
        for r in range(1, 4):
            arrived(x_recv.at[b, r], x_rsem.at[b, r])
            v = v + x_recv[b, r].astype(F32)
        for n, (sy, t) in reversed(list(enumerate(yrel))):
            two = [v[sy * 8:sy * 8 + 8, t * 256 + e * 128:t * 256 + e * 128 + 128] for e in range(2)]
            both = jnp.concatenate(two, 0)
            if n == 0:
                own[b] = both
            else:
                y_send[b, n] = both.astype(BF16)
                send(
                    y_send.at[b, n], y_recv.at[b, n], y_ssem.at[b, n], y_rsem.at[b, n],
                    at(dyh=sy, dyl=t),
                )

    def send_z(b):
        v = own[b]
        for n in range(1, 8):
            arrived(y_recv.at[b, n], y_rsem.at[b, n])
            v = v + y_recv[b, n].astype(F32)
        for e in range(2):
            q = 2 * b + e
            z_send[q] = v[e * 8:e * 8 + 8]
            if q:
                send(z_send.at[q], z_recv.at[q], z_ssem.at[q], z_rsem.at[q], at(dz=q))

    for b in range(BLOCKS + 3):
        if b < BLOCKS:
            compute(b)
            send_core(b)
        if 0 <= b - 1 < BLOCKS:
            send_x(b - 1)
        if 0 <= b - 2 < BLOCKS:
            send_y(b - 2)
        if 0 <= b - 3 < BLOCKS:
            send_z(b - 3)

    v = z_send[0]
    for q in range(1, 8):
        arrived(z_recv.at[q], z_rsem.at[q])
        v = v + z_recv[q]
    out_ref[...] = v

    for h in halo:
        h.wait_send()
    for c in sent:
        c.wait_send()


def local(modes, metric, block_map, flags, region_scale):
    total_cells = (
        modes.shape[2] * lax.axis_size("grp") * modes.shape[3] * lax.axis_size("blk") * modes.shape[4]
    )
    norm = float(total_cells) ** (-0.5)
    hbm = pl.BlockSpec(memory_space=pl.ANY)
    dma = pltpu.SemaphoreType.DMA
    scratch = [
        pltpu.VMEM((3, M * CELLS, 128), BF16),
        pltpu.VMEM((3, M * CELLS, 128), F32),
        pltpu.VMEM((3, KS * CELLS, 128), BF16),
        pltpu.VMEM((3 * KS * CELLS, 128), F32),
        pltpu.VMEM((3 * CELLS, 128), F32),
        pltpu.VMEM((CELLS, 128), jnp.int32),
        pltpu.VMEM((CELLS, 128), jnp.int32),
        pltpu.VMEM((CELLS, 9 * KS, 128), F32),
        pltpu.VMEM((M, 3072), BF16),
        pltpu.VMEM((BLOCKS, M, 512), F32),
        pltpu.VMEM((2, 96, 128), BF16),
        pltpu.VMEM((2, 48, 128), BF16),
        pltpu.VMEM((2, 96, 128), BF16),
        pltpu.VMEM((2, 48, 128), BF16),
        pltpu.VMEM((BLOCKS, 128, 512), BF16),
        pltpu.VMEM((BLOCKS, 128, 512), BF16),
        pltpu.VMEM((BLOCKS, 4, 32, 512), BF16),
        pltpu.VMEM((BLOCKS, 4, 32, 512), BF16),
        pltpu.VMEM((BLOCKS, 8, 16, 128), BF16),
        pltpu.VMEM((BLOCKS, 8, 16, 128), BF16),
        pltpu.VMEM((8, 8, 128), F32),
        pltpu.VMEM((8, 8, 128), F32),
        pltpu.VMEM((BLOCKS, 16, 128), F32),
        dma((5,)),
        dma((4,)),
        dma((4,)),
        dma((BLOCKS,)),
        dma((BLOCKS,)),
        dma((BLOCKS, 4)),
        dma((BLOCKS, 4)),
        dma((BLOCKS, 8)),
        dma((BLOCKS, 8)),
        dma((8,)),
        dma((8,)),
    ]
    summed = pl.pallas_call(
        functools.partial(kernel, norm),
        out_shape=jax.ShapeDtypeStruct((8, 128), F32),
        in_specs=[hbm, hbm, hbm, hbm, pl.BlockSpec(memory_space=pltpu.SMEM)],
        out_specs=pl.BlockSpec(memory_space=pltpu.VMEM),
        scratch_shapes=scratch,
        compiler_params=pltpu.CompilerParams(
            collective_id=0, has_side_effects=True, vmem_limit_bytes=40 * 1024 * 1024
        ),
        cost_estimate=pl.CostEstimate(
            flops=2 * 2048 * 3072 * 256, bytes_accessed=2 * 1024 * 1024, transcendentals=0
        ),
    )(
        modes.reshape(3, M * CELLS, 128),
        metric.reshape(3 * CELLS, 128),
        block_map.reshape(CELLS, 128),
        flags.reshape(CELLS, 128),
        region_scale,
    )
    return summed.reshape(8, KS, 16).transpose(1, 2, 0)


def solution(mesh):
    return jax.shard_map(
        local,
        mesh=mesh,
        in_specs=(
            P(None, None, "grp", "blk", None),
            P(None, "grp", "blk", None),
            P("grp", "blk", None),
            P("grp", "blk", None),
            P(),
        ),
        out_specs=P(None, "grp", "blk"),
        check_vma=False,
    )
```

```python
import functools

import jax
import jax.numpy as jnp
from jax import lax
from jax.experimental import pallas as pl
from jax.experimental.pallas import tpu as pltpu
from jax.sharding import PartitionSpec as P

KS = 8
M = 256
CELLS = 8
NX, NY = 2, 4
F32, BF16 = jnp.float32, jnp.bfloat16
MESH = pl.DeviceIdType.MESH
Z_OF = ((4, 3), (5, 2), (6, 7), (1, 0))
BLOCKS = len(Z_OF)


def kernel(
    norm,
    modes_hbm, metric_hbm, map_hbm, flags_hbm, scale_ref,
    out_ref,
    nat, natf, slab, slabf, met, bmap, flg, gtab, bmat, first, rest, pacc,
    hx_send, hy_send, hx_recv, hy_recv,
    c_send, c_recv, x_send, x_recv, z_send, z_recv,
    in_sem, h_ssem, h_rsem, c_ssem, c_rsem, x_ssem, x_rsem, z_ssem, z_rsem,
):
    grp = lax.axis_index("grp")
    blk = lax.axis_index("blk")
    z, y_lo = grp % 8, grp // 8
    core, y_hi, x = blk % 2, (blk // 2) % 4, blk // 8

    def at(dx=0, dyh=0, dyl=0, dz=0, dc=0):
        g = ((y_lo + dyl) % 2) * 8 + (z + dz) % 8
        b = ((x + dx) % 4) * 8 + ((y_hi + dyh) % 4) * 2 + (core + dc) % 2
        return (g, b)

    halo_to = [
        ((grp + 1) % 16, blk),
        ((grp + 15) % 16, blk),
        (grp, (blk + 1) % 32),
        (grp, (blk + 31) % 32),
    ]
    x_rel = [(r, t) for r in range(4) for t in range(2)]
    z_rel = [(q, s) for q in range(8) for s in range(4)]
    partners = list(halo_to)
    partners.append(at(dc=1))
    partners += [at(dx=r, dyl=t) for r, t in x_rel[1:]]
    partners += [at(dz=q, dyh=s) for q, s in z_rel[1:]]

    barrier = pltpu.get_barrier_semaphore()
    for p in partners:
        pl.semaphore_signal(barrier, inc=1, device_id=p, device_id_type=MESH)

    loads = [
        pltpu.make_async_copy(modes_hbm.at[:, pl.ds(0, KS * CELLS), :], slab, in_sem.at[0]),
        pltpu.make_async_copy(metric_hbm, met, in_sem.at[1]),
        pltpu.make_async_copy(map_hbm, bmap, in_sem.at[2]),
        pltpu.make_async_copy(flags_hbm, flg, in_sem.at[3]),
        pltpu.make_async_copy(modes_hbm, nat, in_sem.at[4]),
    ]
    for c in loads:
        c.start()

    loads[0].wait()
    for c in range(3):
        slabf[c * 64:(c + 1) * 64, :] = slab[c].astype(F32)

    def tile(c, row):
        return slabf[pl.ds(c * 64 + row, KS, stride=CELLS), :]

    s = {(c, row): tile(c, row) for c in range(3) for row in range(CELLS)}
    for side, xi in ((0, 1), (1, 0)):
        for c in range(3):
            for yp in range(2):
                a = s[c, xi * NY + 2 * yp]
                b = s[c, xi * NY + 2 * yp + 1]
                at_row = (c * 2 + yp) * 16
                hx_send[side, at_row:at_row + 16, :] = jnp.concatenate([a, b], 0).astype(BF16)
    for side, yi in ((0, 3), (1, 0)):
        for c in range(3):
            a, b = s[c, yi], s[c, NY + yi]
            hy_send[side, c * 16:c * 16 + 16, :] = jnp.concatenate([a, b], 0).astype(BF16)

    pl.semaphore_wait(barrier, len(partners))

    def remote(src, dst, ssem, rsem, to):
        return pltpu.make_async_remote_copy(
            src_ref=src, dst_ref=dst, send_sem=ssem, recv_sem=rsem,
            device_id=to, device_id_type=MESH,
        )

    halo = []
    for n in range(4):
        src, dst = (hx_send, hx_recv) if n < 2 else (hy_send, hy_recv)
        halo.append(remote(src.at[n % 2], dst.at[n % 2], h_ssem.at[n], h_rsem.at[n], halo_to[n]))
        halo[-1].start()

    loads[1].wait()
    loads[2].wait()
    loads[3].wait()
    region = bmap[...]
    scale = jnp.zeros((CELLS, 128), F32)
    for r in range(16):
        scale = jnp.where(region == r, scale_ref[r], scale)
    kinds = flg[...]
    fluid = jnp.where(kinds == 0, F32(1.0), jnp.where(kinds == 1, F32(0.0), F32(0.5)))
    m = [met[d * CELLS:(d + 1) * CELLS, :] for d in range(3)]
    weight = scale * fluid * norm / (m[0] * m[1] * m[2])
    half = [0.5 * weight * m[d] for d in range(3)]

    loads[4].wait()

    def widen(n, _):
        rows = pl.ds(pl.multiple_of(n * 256, 256), 256)
        for c in range(3):
            natf[c, rows, :] = nat[c, rows, :].astype(F32)
        return 0

    lax.fori_loop(0, 8, widen, 0)

    def spread(n, _):
        cc = (core + n // 4) % 2
        xx = (x + n % 4) % 4
        for pair in range(2):
            starts = []
            for e in range(2):
                yy = (y_hi + 2 * pair + e) % 4
                starts.append((xx * 8 + yy * 2 + cc) * (8 * CELLS))
            rows = pl.ds(pl.multiple_of(n * 32 + pair * 16, 16), 16)
            for d in range(3):
                for row in range(CELLS):
                    both = jnp.concatenate(
                        [natf[d, pl.ds(st + row, 8, stride=CELLS), :] for st in starts], 0
                    )
                    col = ((d + 1) % 3 * CELLS + row) * 128
                    bmat[rows, col:col + 128] = both.astype(BF16)
        return 0

    lax.fori_loop(0, 8, spread, 0)

    lane = lax.broadcasted_iota(jnp.int32, (KS, 128), 1)

    def put(d, c, row, diff):
        base = (d * 3 + c) * KS
        gtab[row, base:base + KS, :] = diff * half[d][row:row + 1, :]

    for c in range(3):
        for row in range(CELLS):
            v = s[c, row]
            after = jnp.where(lane == 127, F32(0.0), pltpu.roll(v, 127, 1))
            before = jnp.where(lane == 0, F32(0.0), pltpu.roll(v, 1, 1))
            put(2, c, row, after - before)

    def fill(ref, b, col, d, row):
        bases = []
        for t in range(2):
            for q in Z_OF[b]:
                bases.append((((y_lo + t) % 2) * 8 + (z + q) % 8) * (16 * CELLS))
        a = [
            jnp.concatenate(
                [natf[c, pl.ds(st + row, 16, stride=CELLS), :] for st in bases], 0
            )
            for c in range(3)
        ]
        for k in range(KS):
            g = [gtab[row, (d * 3 + c) * KS + k:(d * 3 + c) * KS + k + 1, :] for c in range(3)]
            tested = (a[0] * g[0] + a[1] * g[1] + a[2] * g[2]).astype(BF16)
            for p in range(4):
                to = p * 128 + k * 16
                ref[b, to:to + 16, col:col + 128] = tested[p * 16:p * 16 + 16]

    def times(cols, tested):
        return lax.dot_general(
            bmat[:, cols], tested, (((1,), (1,)), ((), ())), preferred_element_type=F32
        )

    for b in range(BLOCKS):
        for row in range(CELLS):
            fill(first, b, row * 128, 2, row)
    for b in range(BLOCKS):
        pacc[b] = times(slice(0, 1024), first[b])

    for h in halo:
        h.wait_recv()
    keep = [
        jnp.where(grp > 0, F32(1.0), F32(0.0)),
        jnp.where(grp < 15, F32(1.0), F32(0.0)),
        jnp.where(blk > 0, F32(1.0), F32(0.0)),
        jnp.where(blk < 31, F32(1.0), F32(0.0)),
    ]
    for c in range(3):
        xs = [[None] * NY, [None] * NY]
        for side in range(2):
            for yp in range(2):
                at_row = (c * 2 + yp) * 16
                both = hx_recv[side, at_row:at_row + 16, :].astype(F32) * keep[side]
                xs[side][2 * yp], xs[side][2 * yp + 1] = both[:8], both[8:]
        ys = []
        for side in range(2):
            both = hy_recv[side, c * 16:c * 16 + 16, :].astype(F32) * keep[2 + side]
            ys.append((both[:8], both[8:]))
        for xi in range(NX):
            for yi in range(NY):
                row = xi * NY + yi
                hi = s[c, row + NY] if xi == 0 else xs[1][yi]
                lo = s[c, row - NY] if xi == 1 else xs[0][yi]
                put(0, c, row, hi - lo)
                hi = s[c, row + 1] if yi < NY - 1 else ys[1][xi]
                lo = s[c, row - 1] if yi > 0 else ys[0][xi]
                put(1, c, row, hi - lo)

    def fill_rest(b):
        for d in range(2):
            for row in range(CELLS):
                fill(rest, b, (d * CELLS + row) * 128, d, row)

    def remote_to(src, dst, ssem, rsem, **rel):
        remote(src, dst, ssem, rsem, at(**rel)).start()

    def done(ref, sem):
        pltpu.make_async_copy(ref, ref, sem).wait()

    def send_core(b):
        c_send[b] = pacc[b, 128:256, :].astype(BF16)
        remote_to(c_send.at[b], c_recv.at[b], c_ssem.at[b], c_rsem.at[b], dc=1)

    def send_x(b):
        done(c_recv.at[b], c_rsem.at[b])
        for r, t in sorted(x_rel, key=lambda p: -(p[0] == 2) * 2 - (p[0] > 0) - p[1]):
            rows, cols = slice(r * 32, r * 32 + 32), slice(t * 256, t * 256 + 256)
            v = pacc[b, rows, cols] + c_recv[b, rows, cols].astype(F32)
            n = (r * 2 + t) * 32
            if n == 0:
                pacc[b, rows, cols] = v
            else:
                x_send[b, n:n + 32, :] = v.astype(BF16)
                part = pl.ds(n, 32)
                remote_to(
                    x_send.at[b, part], x_recv.at[b, part], x_ssem.at[b], x_rsem.at[b],
                    dx=r, dyl=t,
                )

    def send_z(b):
        done(x_recv.at[b, pl.ds(32, 224)], x_rsem.at[b])
        v = pacc[b, 0:32, 0:256]
        for n in range(1, 8):
            v = v + x_recv[b, n * 32:n * 32 + 32, :].astype(F32)
        for e in range(2):
            for sy in (2, 1, 3, 0):
                n = (e * 4 + 3 - sy) * 8
                z_send[b, n:n + 8, :] = v[sy * 8:sy * 8 + 8, e * 128:e * 128 + 128]
                if Z_OF[b][e] or sy:
                    part = pl.ds(n, 8)
                    remote_to(
                        z_send.at[b, part], z_recv.at[b, part], z_ssem.at[b], z_rsem.at[b],
                        dz=Z_OF[b][e], dyh=sy,
                    )

    fill_rest(0)
    for b in range(BLOCKS + 2):
        if b + 1 < BLOCKS:
            fill_rest(b + 1)
        if b < BLOCKS:
            pacc[b] = pacc[b] + times(slice(1024, 3072), rest[b])
            send_core(b)
        if 0 <= b - 1 < BLOCKS:
            send_x(b - 1)
        if 0 <= b - 2 < BLOCKS:
            send_z(b - 2)

    last = BLOCKS - 1
    v = z_send[last, 56:64, :]
    for b in range(BLOCKS):
        if b == last:
            done(z_recv.at[b, pl.ds(0, 56)], z_rsem.at[b])
        else:
            done(z_recv.at[b], z_rsem.at[b])
        for n in range(7 if b == last else 8):
            v = v + z_recv[b, n * 8:n * 8 + 8, :]
    out_ref[...] = v

    for h in halo:
        h.wait_send()
    for b in range(BLOCKS):
        done(c_send.at[b], c_ssem.at[b])
        done(x_send.at[b, pl.ds(32, 224)], x_ssem.at[b])
        done(z_send.at[b, pl.ds(0, 56 if b == last else 64)], z_ssem.at[b])


def local(modes, metric, block_map, flags, region_scale):
    total_cells = (
        modes.shape[2] * lax.axis_size("grp") * modes.shape[3] * lax.axis_size("blk") * modes.shape[4]
    )
    norm = float(total_cells) ** (-0.5)
    hbm = pl.BlockSpec(memory_space=pl.ANY)
    dma = pltpu.SemaphoreType.DMA
    scratch = [
        pltpu.VMEM((3, M * CELLS, 128), BF16),
        pltpu.VMEM((3, M * CELLS, 128), F32),
        pltpu.VMEM((3, KS * CELLS, 128), BF16),
        pltpu.VMEM((3 * KS * CELLS, 128), F32),
        pltpu.VMEM((3 * CELLS, 128), F32),
        pltpu.VMEM((CELLS, 128), jnp.int32),
        pltpu.VMEM((CELLS, 128), jnp.int32),
        pltpu.VMEM((CELLS, 9 * KS, 128), F32),
        pltpu.VMEM((M, 3072), BF16),
        pltpu.VMEM((BLOCKS, 512, 1024), BF16),
        pltpu.VMEM((BLOCKS, 512, 2048), BF16),
        pltpu.VMEM((BLOCKS, M, 512), F32),
        pltpu.VMEM((2, 96, 128), BF16),
        pltpu.VMEM((2, 48, 128), BF16),
        pltpu.VMEM((2, 96, 128), BF16),
        pltpu.VMEM((2, 48, 128), BF16),
        pltpu.VMEM((BLOCKS, 128, 512), BF16),
        pltpu.VMEM((BLOCKS, 128, 512), BF16),
        pltpu.VMEM((BLOCKS, 256, 256), BF16),
        pltpu.VMEM((BLOCKS, 256, 256), BF16),
        pltpu.VMEM((BLOCKS, 64, 128), F32),
        pltpu.VMEM((BLOCKS, 64, 128), F32),
        dma((5,)),
        dma((4,)),
        dma((4,)),
        dma((BLOCKS,)),
        dma((BLOCKS,)),
        dma((BLOCKS,)),
        dma((BLOCKS,)),
        dma((BLOCKS,)),
        dma((BLOCKS,)),
    ]
    summed = pl.pallas_call(
        functools.partial(kernel, norm),
        out_shape=jax.ShapeDtypeStruct((8, 128), F32),
        in_specs=[hbm, hbm, hbm, hbm, pl.BlockSpec(memory_space=pltpu.SMEM)],
        out_specs=pl.BlockSpec(memory_space=pltpu.VMEM),
        scratch_shapes=scratch,
        compiler_params=pltpu.CompilerParams(
            collective_id=0, has_side_effects=True, vmem_limit_bytes=63 * 1024 * 1024
        ),
        cost_estimate=pl.CostEstimate(
            flops=2 * 2048 * 3072 * 256, bytes_accessed=2 * 1024 * 1024, transcendentals=0
        ),
    )(
        modes.reshape(3, M * CELLS, 128),
        metric.reshape(3 * CELLS, 128),
        block_map.reshape(CELLS, 128),
        flags.reshape(CELLS, 128),
        region_scale,
    )
    return summed.reshape(8, KS, 16).transpose(1, 2, 0)


def solution(mesh):
    return jax.shard_map(
        local,
        mesh=mesh,
        in_specs=(
            P(None, None, "grp", "blk", None),
            P(None, "grp", "blk", None),
            P("grp", "blk", None),
            P("grp", "blk", None),
            P(),
        ),
        out_specs=P(None, "grp", "blk"),
        check_vma=False,
    )
```

```python
import functools

import jax
import jax.numpy as jnp
from jax import lax
from jax.experimental import pallas as pl
from jax.experimental.pallas import tpu as pltpu
from jax.sharding import PartitionSpec as P

KS = 8
M = 256
CELLS = 8
NX, NY = 2, 4
F32, BF16 = jnp.float32, jnp.bfloat16
MESH = pl.DeviceIdType.MESH
Z_OF = ((4, 3), (5, 2), (6, 7), (1, 0))
BLOCKS = len(Z_OF)


def kernel(
    norm,
    modes_hbm, metric_hbm, map_hbm, flags_hbm, scale_ref,
    out_ref,
    nat, natf, slab, slabf, met, bmap, flg, gtab, bmat, first, rest, pacc,
    hx_send, hy_send, hx_recv, hy_recv,
    c_send, c_recv, x_send, x_recv, z_send, z_recv,
    in_sem, h_ssem, h_rsem, c_ssem, c_rsem, x_ssem, x_rsem, z_ssem, z_rsem,
):
    grp = lax.axis_index("grp")
    blk = lax.axis_index("blk")
    z, y_lo = grp % 8, grp // 8
    core, y_hi, x = blk % 2, (blk // 2) % 4, blk // 8

    def at(dx=0, dyh=0, dyl=0, dz=0, dc=0):
        g = ((y_lo + dyl) % 2) * 8 + (z + dz) % 8
        b = ((x + dx) % 4) * 8 + ((y_hi + dyh) % 4) * 2 + (core + dc) % 2
        return (g, b)

    halo_to = [
        ((grp + 1) % 16, blk),
        ((grp + 15) % 16, blk),
        (grp, (blk + 1) % 32),
        (grp, (blk + 31) % 32),
    ]
    x_rel = [(r, t) for r in range(4) for t in range(2)]
    z_rel = [(q, s) for q in range(8) for s in range(4)]
    partners = list(halo_to)
    partners.append(at(dc=1))
    partners += [at(dx=r, dyl=t) for r, t in x_rel[1:]]
    partners += [at(dz=q, dyh=s) for q, s in z_rel[1:]]

    barrier = pltpu.get_barrier_semaphore()
    for p in partners:
        pl.semaphore_signal(barrier, inc=1, device_id=p, device_id_type=MESH)

    loads = [
        pltpu.make_async_copy(modes_hbm.at[:, pl.ds(0, KS * CELLS), :], slab, in_sem.at[0]),
        pltpu.make_async_copy(metric_hbm, met, in_sem.at[1]),
        pltpu.make_async_copy(map_hbm, bmap, in_sem.at[2]),
        pltpu.make_async_copy(flags_hbm, flg, in_sem.at[3]),
        pltpu.make_async_copy(modes_hbm, nat, in_sem.at[4]),
    ]
    for c in loads:
        c.start()

    loads[0].wait()
    for c in range(3):
        slabf[c * 64:(c + 1) * 64, :] = slab[c].astype(F32)

    def tile(c, row):
        return slabf[pl.ds(c * 64 + row, KS, stride=CELLS), :]

    s = {(c, row): tile(c, row) for c in range(3) for row in range(CELLS)}
    for side, xi in ((0, 1), (1, 0)):
        for c in range(3):
            for yp in range(2):
                a = s[c, xi * NY + 2 * yp]
                b = s[c, xi * NY + 2 * yp + 1]
                at_row = (c * 2 + yp) * 16
                hx_send[side, at_row:at_row + 16, :] = jnp.concatenate([a, b], 0).astype(BF16)
    for side, yi in ((0, 3), (1, 0)):
        for c in range(3):
            a, b = s[c, yi], s[c, NY + yi]
            hy_send[side, c * 16:c * 16 + 16, :] = jnp.concatenate([a, b], 0).astype(BF16)

    pl.semaphore_wait(barrier, len(partners))

    def remote(src, dst, ssem, rsem, to):
        return pltpu.make_async_remote_copy(
            src_ref=src, dst_ref=dst, send_sem=ssem, recv_sem=rsem,
            device_id=to, device_id_type=MESH,
        )

    halo = []
    for n in range(4):
        src, dst = (hx_send, hx_recv) if n < 2 else (hy_send, hy_recv)
        halo.append(remote(src.at[n % 2], dst.at[n % 2], h_ssem.at[n], h_rsem.at[n], halo_to[n]))
        halo[-1].start()

    loads[1].wait()
    loads[2].wait()
    loads[3].wait()
    region = bmap[...]
    scale = jnp.zeros((CELLS, 128), F32)
    for r in range(16):
        scale = jnp.where(region == r, scale_ref[r], scale)
    kinds = flg[...]
    fluid = jnp.where(kinds == 0, F32(1.0), jnp.where(kinds == 1, F32(0.0), F32(0.5)))
    m = [met[d * CELLS:(d + 1) * CELLS, :] for d in range(3)]
    weight = scale * fluid * norm / (m[0] * m[1] * m[2])
    half = [0.5 * weight * m[d] for d in range(3)]

    loads[4].wait()

    def widen(n, _):
        rows = pl.ds(pl.multiple_of(n * 256, 256), 256)
        for c in range(3):
            natf[c, rows, :] = nat[c, rows, :].astype(F32)
        return 0

    lax.fori_loop(0, 8, widen, 0)

    def spread(n, _):
        cc = (core + n // 4) % 2
        xx = (x + n % 4) % 4
        for pair in range(2):
            starts = []
            for e in range(2):
                yy = (y_hi + 2 * pair + e) % 4
                starts.append((xx * 8 + yy * 2 + cc) * (8 * CELLS))
            rows = pl.ds(pl.multiple_of(n * 32 + pair * 16, 16), 16)
            for d in range(3):
                for row in range(CELLS):
                    both = jnp.concatenate(
                        [natf[d, pl.ds(st + row, 8, stride=CELLS), :] for st in starts], 0
                    )
                    if d == 2:
                        col = row * 128
                    else:
                        col = 1024 + (row // 2) * 512 + d * 256 + (row % 2) * 128
                    bmat[rows, col:col + 128] = both.astype(BF16)
        return 0

    lax.fori_loop(0, 8, spread, 0)

    lane = lax.broadcasted_iota(jnp.int32, (KS, 128), 1)

    def put(d, c, row, diff):
        base = (d * 3 + c) * KS
        gtab[row, base:base + KS, :] = diff * half[d][row:row + 1, :]

    for c in range(3):
        for row in range(CELLS):
            v = s[c, row]
            after = jnp.where(lane == 127, F32(0.0), pltpu.roll(v, 127, 1))
            before = jnp.where(lane == 0, F32(0.0), pltpu.roll(v, 1, 1))
            put(2, c, row, after - before)

    wide = [256 * len(qs) for qs in Z_OF]

    def tested(b, ds, pair):
        bases = []
        for t in range(2):
            for q in Z_OF[b]:
                bases.append((((y_lo + t) % 2) * 8 + (z + q) % 8) * (16 * CELLS))

        def rows_of(d):
            halves = []
            for e in range(2):
                row = pair * 2 + e
                a = [
                    jnp.concatenate(
                        [natf[c, pl.ds(st + row, 16, stride=CELLS), :] for st in bases], 0
                    )
                    for c in range(3)
                ]
                per_k = []
                for k in range(KS):
                    g = [gtab[row, pl.ds((d * 3 + c) * KS + k, 1), :] for c in range(3)]
                    per_k.append((a[0] * g[0] + a[1] * g[1] + a[2] * g[2]).astype(BF16))
                halves.append(
                    jnp.concatenate(
                        [
                            per_k[k][p * 16:p * 16 + 16]
                            for p in range(len(bases))
                            for k in range(KS)
                        ],
                        0,
                    )
                )
            return jnp.concatenate(halves, 1)

        return jnp.concatenate([rows_of(d) for d in ds], 1)

    def fill(ref, b, ds):
        width = 256 * len(ds)
        for pair in range(4):
            ref[b, 0:wide[b], pair * width:pair * width + width] = tested(b, ds, pair)

    def times(cols, tested):
        return lax.dot_general(
            bmat[:, cols], tested, (((1,), (1,)), ((), ())), preferred_element_type=F32
        )

    for b in range(BLOCKS):
        fill(first, b, (2,))
        pacc[b, :, 0:wide[b]] = times(slice(0, 1024), first[b, 0:wide[b], :])

    for h in halo:
        h.wait_recv()
    keep = [
        jnp.where(grp > 0, F32(1.0), F32(0.0)),
        jnp.where(grp < 15, F32(1.0), F32(0.0)),
        jnp.where(blk > 0, F32(1.0), F32(0.0)),
        jnp.where(blk < 31, F32(1.0), F32(0.0)),
    ]
    for c in range(3):
        xs = [[None] * NY, [None] * NY]
        for side in range(2):
            for yp in range(2):
                at_row = (c * 2 + yp) * 16
                both = hx_recv[side, at_row:at_row + 16, :].astype(F32) * keep[side]
                xs[side][2 * yp], xs[side][2 * yp + 1] = both[:8], both[8:]
        ys = []
        for side in range(2):
            both = hy_recv[side, c * 16:c * 16 + 16, :].astype(F32) * keep[2 + side]
            ys.append((both[:8], both[8:]))
        for xi in range(NX):
            for yi in range(NY):
                row = xi * NY + yi
                hi = s[c, row + NY] if xi == 0 else xs[1][yi]
                lo = s[c, row - NY] if xi == 1 else xs[0][yi]
                put(0, c, row, hi - lo)
                hi = s[c, row + 1] if yi < NY - 1 else ys[1][xi]
                lo = s[c, row - 1] if yi > 0 else ys[0][xi]
                put(1, c, row, hi - lo)

    def remote_to(src, dst, ssem, rsem, **rel):
        remote(src, dst, ssem, rsem, at(**rel)).start()

    def done(ref, sem):
        pltpu.make_async_copy(ref, ref, sem).wait()

    def core_part(ref, b):
        return ref.at[b, :, pl.ds(0, wide[b])]

    def x_part(ref, b, n=1, count=7):
        return ref.at[b, pl.ds(n * 32, count * 32), pl.ds(0, wide[b] // 2)]

    def z_part(ref, b, n, count):
        return ref.at[b, pl.ds(n * 8, count * 8)]

    def send_core(b):
        w = wide[b]
        c_send[b, :, 0:w] = pacc[b, 128:256, 0:w].astype(BF16)
        remote_to(core_part(c_send, b), core_part(c_recv, b), c_ssem.at[b], c_rsem.at[b], dc=1)

    def send_x(b):
        done(core_part(c_recv, b), c_rsem.at[b])
        h = wide[b] // 2
        for r, t in ((2, 1), (2, 0), (1, 1), (3, 1), (1, 0), (3, 0), (0, 1), (0, 0)):
            rows, cols = slice(r * 32, r * 32 + 32), slice(t * h, t * h + h)
            v = pacc[b, rows, cols] + c_recv[b, rows, cols].astype(F32)
            n = r * 2 + t
            if n == 0:
                pacc[b, rows, cols] = v
            else:
                x_send[b, n * 32:n * 32 + 32, 0:h] = v.astype(BF16)
                remote_to(
                    x_part(x_send, b, n, 1), x_part(x_recv, b, n, 1), x_ssem.at[b], x_rsem.at[b],
                    dx=r, dyl=t,
                )

    def send_z(b):
        done(x_part(x_recv, b), x_rsem.at[b])
        h = wide[b] // 2
        v = pacc[b, 0:32, 0:h]
        for n in range(1, 8):
            v = v + x_recv[b, n * 32:n * 32 + 32, 0:h].astype(F32)
        for e, q in enumerate(Z_OF[b]):
            for sy in (2, 1, 3, 0):
                n = e * 4 + 3 - sy
                z_send[b, n * 8:n * 8 + 8, :] = v[sy * 8:sy * 8 + 8, e * 128:e * 128 + 128]
                if q or sy:
                    remote_to(
                        z_part(z_send, b, n, 1), z_part(z_recv, b, n, 1), z_ssem.at[b], z_rsem.at[b],
                        dz=q, dyh=sy,
                    )

    for b in range(BLOCKS):
        fill(rest, b, (0, 1))
        w = wide[b]
        pacc[b, :, 0:w] = pacc[b, :, 0:w] + times(slice(1024, 3072), rest[b, 0:w, :])
        send_core(b)
        if b:
            send_x(b - 1)
    send_x(BLOCKS - 1)
    for b in range(BLOCKS):
        send_z(b)

    last = BLOCKS - 1
    got = [4 * len(qs) - (b == last) for b, qs in enumerate(Z_OF)]
    v = z_send[last, got[last] * 8:got[last] * 8 + 8, :]
    for b in range(BLOCKS):
        done(z_part(z_recv, b, 0, got[b]), z_rsem.at[b])
        for n in range(got[b]):
            v = v + z_recv[b, n * 8:n * 8 + 8, :]
    out_ref[...] = v

    for h in halo:
        h.wait_send()
    for b in range(BLOCKS):
        done(core_part(c_send, b), c_ssem.at[b])
        done(x_part(x_send, b), x_ssem.at[b])
        done(z_part(z_send, b, 0, got[b]), z_ssem.at[b])


def local(modes, metric, block_map, flags, region_scale):
    total_cells = (
        modes.shape[2] * lax.axis_size("grp") * modes.shape[3] * lax.axis_size("blk") * modes.shape[4]
    )
    norm = float(total_cells) ** (-0.5)
    hbm = pl.BlockSpec(memory_space=pl.ANY)
    dma = pltpu.SemaphoreType.DMA
    scratch = [
        pltpu.VMEM((3, M * CELLS, 128), BF16),
        pltpu.VMEM((3, M * CELLS, 128), F32),
        pltpu.VMEM((3, KS * CELLS, 128), BF16),
        pltpu.VMEM((3 * KS * CELLS, 128), F32),
        pltpu.VMEM((3 * CELLS, 128), F32),
        pltpu.VMEM((CELLS, 128), jnp.int32),
        pltpu.VMEM((CELLS, 128), jnp.int32),
        pltpu.VMEM((CELLS, 9 * KS, 128), F32),
        pltpu.VMEM((M, 3072), BF16),
        pltpu.VMEM((BLOCKS, 512, 1024), BF16),
        pltpu.VMEM((BLOCKS, 512, 2048), BF16),
        pltpu.VMEM((BLOCKS, M, 512), F32),
        pltpu.VMEM((2, 96, 128), BF16),
        pltpu.VMEM((2, 48, 128), BF16),
        pltpu.VMEM((2, 96, 128), BF16),
        pltpu.VMEM((2, 48, 128), BF16),
        pltpu.VMEM((BLOCKS, 128, 512), BF16),
        pltpu.VMEM((BLOCKS, 128, 512), BF16),
        pltpu.VMEM((BLOCKS, 256, 256), BF16),
        pltpu.VMEM((BLOCKS, 256, 256), BF16),
        pltpu.VMEM((BLOCKS, 64, 128), F32),
        pltpu.VMEM((BLOCKS, 64, 128), F32),
        dma((5,)),
        dma((4,)),
        dma((4,)),
        dma((BLOCKS,)),
        dma((BLOCKS,)),
        dma((BLOCKS,)),
        dma((BLOCKS,)),
        dma((BLOCKS,)),
        dma((BLOCKS,)),
    ]
    summed = pl.pallas_call(
        functools.partial(kernel, norm),
        out_shape=jax.ShapeDtypeStruct((8, 128), F32),
        in_specs=[hbm, hbm, hbm, hbm, pl.BlockSpec(memory_space=pltpu.SMEM)],
        out_specs=pl.BlockSpec(memory_space=pltpu.VMEM),
        scratch_shapes=scratch,
        compiler_params=pltpu.CompilerParams(
            collective_id=0, has_side_effects=True, vmem_limit_bytes=63 * 1024 * 1024
        ),
        cost_estimate=pl.CostEstimate(
            flops=2 * 2048 * 3072 * 256, bytes_accessed=2 * 1024 * 1024, transcendentals=0
        ),
    )(
        modes.reshape(3, M * CELLS, 128),
        metric.reshape(3 * CELLS, 128),
        block_map.reshape(CELLS, 128),
        flags.reshape(CELLS, 128),
        region_scale,
    )
    return summed.reshape(8, KS, 16).transpose(1, 2, 0)


def solution(mesh):
    return jax.shard_map(
        local,
        mesh=mesh,
        in_specs=(
            P(None, None, "grp", "blk", None),
            P(None, "grp", "blk", None),
            P("grp", "blk", None),
            P("grp", "blk", None),
            P(),
        ),
        out_specs=P(None, "grp", "blk"),
        check_vma=False,
    )
```

```python
import functools

import jax
import jax.numpy as jnp
from jax import lax
from jax.experimental import pallas as pl
from jax.experimental.pallas import tpu as pltpu
from jax.sharding import PartitionSpec as P

KS = 8
M = 256
CELLS = 8
NX, NY = 2, 4
F32, BF16 = jnp.float32, jnp.bfloat16
MESH = pl.DeviceIdType.MESH
Z_OF = ((4, 3), (5, 2), (6, 7), (1, 0))
BLOCKS = len(Z_OF)
INNER = tuple(((2, r), (2, r + 1), (1, r + 1 if r % 4 == 0 else r)) for r in (0, 2, 4, 6))
OUTER = tuple(((0, r), (0, r + 1), (1, r if r % 4 == 0 else r + 1)) for r in (0, 2, 4, 6))
ORDER = [dr for group in INNER + OUTER for dr in group]


def kernel(
    norm,
    modes_hbm, metric_hbm, map_hbm, flags_hbm, scale_ref,
    out_ref,
    nat, natf, slab, slabf, met, bmap, flg, gtab, bmat, first, rest, pacc,
    hx_send, hy_send, hx_recv, hy_recv,
    c_send, c_recv, x_send, x_recv, z_send, z_recv,
    in_sem, h_ssem, h_rsem, c_ssem, c_rsem, x_ssem, x_rsem, z_ssem, z_rsem,
):
    grp = lax.axis_index("grp")
    blk = lax.axis_index("blk")
    z, y_lo = grp % 8, grp // 8
    core, y_hi, x = blk % 2, (blk // 2) % 4, blk // 8

    def at(dx=0, dyh=0, dyl=0, dz=0, dc=0):
        g = ((y_lo + dyl) % 2) * 8 + (z + dz) % 8
        b = ((x + dx) % 4) * 8 + ((y_hi + dyh) % 4) * 2 + (core + dc) % 2
        return (g, b)

    halo_to = [
        ((grp + 1) % 16, blk),
        ((grp + 15) % 16, blk),
        (grp, (blk + 1) % 32),
        (grp, (blk + 31) % 32),
    ]
    x_rel = [(r, t) for r in range(4) for t in range(2)]
    z_rel = [(q, s) for q in range(8) for s in range(4)]
    partners = list(halo_to)
    partners.append(at(dc=1))
    partners += [at(dx=r, dyl=t) for r, t in x_rel[1:]]
    partners += [at(dz=q, dyh=s) for q, s in z_rel[1:]]

    barrier = pltpu.get_barrier_semaphore()
    for p in partners:
        pl.semaphore_signal(barrier, inc=1, device_id=p, device_id_type=MESH)

    loads = [
        pltpu.make_async_copy(modes_hbm.at[:, pl.ds(0, KS * CELLS), :], slab, in_sem.at[0]),
        pltpu.make_async_copy(metric_hbm, met, in_sem.at[1]),
        pltpu.make_async_copy(map_hbm, bmap, in_sem.at[2]),
        pltpu.make_async_copy(flags_hbm, flg, in_sem.at[3]),
        pltpu.make_async_copy(modes_hbm, nat, in_sem.at[4]),
    ]
    for c in loads:
        c.start()

    loads[0].wait()
    for c in range(3):
        slabf[c * 64:(c + 1) * 64, :] = slab[c].astype(F32)

    def tile(c, row):
        return slabf[pl.ds(c * 64 + row, KS, stride=CELLS), :]

    s = {(c, row): tile(c, row) for c in range(3) for row in range(CELLS)}
    for side, xi in ((0, 1), (1, 0)):
        for c in range(3):
            for yp in range(2):
                a = s[c, xi * NY + 2 * yp]
                b = s[c, xi * NY + 2 * yp + 1]
                at_row = (c * 2 + yp) * 16
                hx_send[side, at_row:at_row + 16, :] = jnp.concatenate([a, b], 0).astype(BF16)
    for side, yi in ((0, 3), (1, 0)):
        for c in range(3):
            a, b = s[c, yi], s[c, NY + yi]
            hy_send[side, c * 16:c * 16 + 16, :] = jnp.concatenate([a, b], 0).astype(BF16)

    pl.semaphore_wait(barrier, len(partners))

    def remote(src, dst, ssem, rsem, to):
        return pltpu.make_async_remote_copy(
            src_ref=src, dst_ref=dst, send_sem=ssem, recv_sem=rsem,
            device_id=to, device_id_type=MESH,
        )

    halo = []
    for n in range(4):
        src, dst = (hx_send, hx_recv) if n < 2 else (hy_send, hy_recv)
        halo.append(remote(src.at[n % 2], dst.at[n % 2], h_ssem.at[n], h_rsem.at[n], halo_to[n]))
        halo[-1].start()

    loads[1].wait()
    loads[2].wait()
    loads[3].wait()
    region = bmap[...]
    scale = jnp.zeros((CELLS, 128), F32)
    for r in range(16):
        scale = jnp.where(region == r, scale_ref[r], scale)
    kinds = flg[...]
    fluid = jnp.where(kinds == 0, F32(1.0), jnp.where(kinds == 1, F32(0.0), F32(0.5)))
    m = [met[d * CELLS:(d + 1) * CELLS, :] for d in range(3)]
    weight = scale * fluid * norm / (m[0] * m[1] * m[2])
    half = [0.5 * weight * m[d] for d in range(3)]

    loads[4].wait()

    def widen(n, _):
        rows = pl.ds(pl.multiple_of(n * 256, 256), 256)
        for c in range(3):
            natf[c, rows, :] = nat[c, rows, :].astype(F32)
        return 0

    lax.fori_loop(0, 8, widen, 0)

    def spread(n, _):
        cc = (core + n // 4) % 2
        xx = (x + n % 4) % 4
        for pair in range(2):
            starts = []
            for e in range(2):
                yy = (y_hi + 2 * pair + e) % 4
                starts.append((xx * 8 + yy * 2 + cc) * (8 * CELLS))
            rows = pl.ds(pl.multiple_of(n * 32 + pair * 16, 16), 16)
            for d in range(3):
                for row in range(CELLS):
                    both = jnp.concatenate(
                        [natf[d, pl.ds(st + row, 8, stride=CELLS), :] for st in starts], 0
                    )
                    col = ORDER.index((d, row)) * 128
                    bmat[rows, col:col + 128] = both.astype(BF16)
        return 0

    lax.fori_loop(0, 8, spread, 0)

    lane = lax.broadcasted_iota(jnp.int32, (KS, 128), 1)

    def put(d, c, row, diff):
        base = (d * 3 + c) * KS
        gtab[row, base:base + KS, :] = diff * half[d][row:row + 1, :]

    for c in range(3):
        for row in range(CELLS):
            v = s[c, row]
            after = jnp.where(lane == 127, F32(0.0), pltpu.roll(v, 127, 1))
            before = jnp.where(lane == 0, F32(0.0), pltpu.roll(v, 1, 1))
            put(2, c, row, after - before)
            if row % NY in (1, 2):
                put(1, c, row, s[c, row + 1] - s[c, row - 1])

    wide = [256 * len(qs) for qs in Z_OF]

    def tested(b, group):
        bases = []
        for t in range(2):
            for q in Z_OF[b]:
                bases.append((((y_lo + t) % 2) * 8 + (z + q) % 8) * (16 * CELLS))

        def columns(d, row):
            a = [
                jnp.concatenate(
                    [natf[c, pl.ds(st + row, 16, stride=CELLS), :] for st in bases], 0
                )
                for c in range(3)
            ]
            per_k = []
            for k in range(KS):
                g = [gtab[row, pl.ds((d * 3 + c) * KS + k, 1), :] for c in range(3)]
                per_k.append((a[0] * g[0] + a[1] * g[1] + a[2] * g[2]).astype(BF16))
            return jnp.concatenate(
                [
                    per_k[k][p * 16:p * 16 + 16]
                    for p in range(len(bases))
                    for k in range(KS)
                ],
                0,
            )

        return jnp.concatenate([columns(d, row) for d, row in group], 1)

    def fill(ref, b, groups):
        for n, group in enumerate(groups):
            ref[b, 0:wide[b], n * 384:n * 384 + 384] = tested(b, group)

    def times(cols, tested):
        return lax.dot_general(
            bmat[:, cols], tested, (((1,), (1,)), ((), ())), preferred_element_type=F32
        )

    for b in range(BLOCKS):
        fill(first, b, INNER)
        pacc[b, :, 0:wide[b]] = times(slice(0, 1536), first[b, 0:wide[b], :])

    for h in halo:
        h.wait_recv()
    keep = [
        jnp.where(grp > 0, F32(1.0), F32(0.0)),
        jnp.where(grp < 15, F32(1.0), F32(0.0)),
        jnp.where(blk > 0, F32(1.0), F32(0.0)),
        jnp.where(blk < 31, F32(1.0), F32(0.0)),
    ]
    for c in range(3):
        xs = [[None] * NY, [None] * NY]
        for side in range(2):
            for yp in range(2):
                at_row = (c * 2 + yp) * 16
                both = hx_recv[side, at_row:at_row + 16, :].astype(F32) * keep[side]
                xs[side][2 * yp], xs[side][2 * yp + 1] = both[:8], both[8:]
        ys = []
        for side in range(2):
            both = hy_recv[side, c * 16:c * 16 + 16, :].astype(F32) * keep[2 + side]
            ys.append((both[:8], both[8:]))
        for xi in range(NX):
            for yi in range(NY):
                row = xi * NY + yi
                hi = s[c, row + NY] if xi == 0 else xs[1][yi]
                lo = s[c, row - NY] if xi == 1 else xs[0][yi]
                put(0, c, row, hi - lo)
                if yi == 0:
                    put(1, c, row, s[c, row + 1] - ys[0][xi])
                elif yi == NY - 1:
                    put(1, c, row, ys[1][xi] - s[c, row - 1])

    def remote_to(src, dst, ssem, rsem, **rel):
        remote(src, dst, ssem, rsem, at(**rel)).start()

    def done(ref, sem):
        pltpu.make_async_copy(ref, ref, sem).wait()

    def core_part(ref, b):
        return ref.at[b, :, pl.ds(0, wide[b])]

    def x_part(ref, b, n=1, count=7):
        return ref.at[b, pl.ds(n * 32, count * 32), pl.ds(0, wide[b] // 2)]

    def z_part(ref, b, n, count):
        return ref.at[b, pl.ds(n * 8, count * 8)]

    def send_core(b):
        w = wide[b]
        c_send[b, :, 0:w] = pacc[b, 128:256, 0:w].astype(BF16)
        remote_to(core_part(c_send, b), core_part(c_recv, b), c_ssem.at[b], c_rsem.at[b], dc=1)

    def send_x(b):
        done(core_part(c_recv, b), c_rsem.at[b])
        h = wide[b] // 2
        for r, t in ((2, 1), (2, 0), (1, 1), (3, 1), (1, 0), (3, 0), (0, 1), (0, 0)):
            rows, cols = slice(r * 32, r * 32 + 32), slice(t * h, t * h + h)
            v = pacc[b, rows, cols] + c_recv[b, rows, cols].astype(F32)
            n = r * 2 + t
            if n == 0:
                pacc[b, rows, cols] = v
            else:
                x_send[b, n * 32:n * 32 + 32, 0:h] = v.astype(BF16)
                remote_to(
                    x_part(x_send, b, n, 1), x_part(x_recv, b, n, 1), x_ssem.at[b], x_rsem.at[b],
                    dx=r, dyl=t,
                )

    def send_z(b):
        done(x_part(x_recv, b), x_rsem.at[b])
        h = wide[b] // 2
        v = pacc[b, 0:32, 0:h]
        for n in range(1, 8):
            v = v + x_recv[b, n * 32:n * 32 + 32, 0:h].astype(F32)
        for e, q in enumerate(Z_OF[b]):
            for sy in (2, 1, 3, 0):
                n = e * 4 + 3 - sy
                z_send[b, n * 8:n * 8 + 8, :] = v[sy * 8:sy * 8 + 8, e * 128:e * 128 + 128]
                if q or sy:
                    remote_to(
                        z_part(z_send, b, n, 1), z_part(z_recv, b, n, 1), z_ssem.at[b], z_rsem.at[b],
                        dz=q, dyh=sy,
                    )

    for b in range(BLOCKS):
        fill(rest, b, OUTER)
        w = wide[b]
        pacc[b, :, 0:w] = pacc[b, :, 0:w] + times(slice(1536, 3072), rest[b, 0:w, :])
        send_core(b)
        if b:
            send_x(b - 1)
    send_x(BLOCKS - 1)
    for b in range(BLOCKS):
        send_z(b)

    last = BLOCKS - 1
    got = [4 * len(qs) - (b == last) for b, qs in enumerate(Z_OF)]
    v = z_send[last, got[last] * 8:got[last] * 8 + 8, :]
    for b in range(BLOCKS):
        done(z_part(z_recv, b, 0, got[b]), z_rsem.at[b])
        for n in range(got[b]):
            v = v + z_recv[b, n * 8:n * 8 + 8, :]
    out_ref[...] = v

    for h in halo:
        h.wait_send()
    for b in range(BLOCKS):
        done(core_part(c_send, b), c_ssem.at[b])
        done(x_part(x_send, b), x_ssem.at[b])
        done(z_part(z_send, b, 0, got[b]), z_ssem.at[b])


def local(modes, metric, block_map, flags, region_scale):
    total_cells = (
        modes.shape[2] * lax.axis_size("grp") * modes.shape[3] * lax.axis_size("blk") * modes.shape[4]
    )
    norm = float(total_cells) ** (-0.5)
    hbm = pl.BlockSpec(memory_space=pl.ANY)
    dma = pltpu.SemaphoreType.DMA
    scratch = [
        pltpu.VMEM((3, M * CELLS, 128), BF16),
        pltpu.VMEM((3, M * CELLS, 128), F32),
        pltpu.VMEM((3, KS * CELLS, 128), BF16),
        pltpu.VMEM((3 * KS * CELLS, 128), F32),
        pltpu.VMEM((3 * CELLS, 128), F32),
        pltpu.VMEM((CELLS, 128), jnp.int32),
        pltpu.VMEM((CELLS, 128), jnp.int32),
        pltpu.VMEM((CELLS, 9 * KS, 128), F32),
        pltpu.VMEM((M, 3072), BF16),
        pltpu.VMEM((BLOCKS, 512, 1536), BF16),
        pltpu.VMEM((BLOCKS, 512, 1536), BF16),
        pltpu.VMEM((BLOCKS, M, 512), F32),
        pltpu.VMEM((2, 96, 128), BF16),
        pltpu.VMEM((2, 48, 128), BF16),
        pltpu.VMEM((2, 96, 128), BF16),
        pltpu.VMEM((2, 48, 128), BF16),
        pltpu.VMEM((BLOCKS, 128, 512), BF16),
        pltpu.VMEM((BLOCKS, 128, 512), BF16),
        pltpu.VMEM((BLOCKS, 256, 256), BF16),
        pltpu.VMEM((BLOCKS, 256, 256), BF16),
        pltpu.VMEM((BLOCKS, 64, 128), F32),
        pltpu.VMEM((BLOCKS, 64, 128), F32),
        dma((5,)),
        dma((4,)),
        dma((4,)),
        dma((BLOCKS,)),
        dma((BLOCKS,)),
        dma((BLOCKS,)),
        dma((BLOCKS,)),
        dma((BLOCKS,)),
        dma((BLOCKS,)),
    ]
    summed = pl.pallas_call(
        functools.partial(kernel, norm),
        out_shape=jax.ShapeDtypeStruct((8, 128), F32),
        in_specs=[hbm, hbm, hbm, hbm, pl.BlockSpec(memory_space=pltpu.SMEM)],
        out_specs=pl.BlockSpec(memory_space=pltpu.VMEM),
        scratch_shapes=scratch,
        compiler_params=pltpu.CompilerParams(
            collective_id=0, has_side_effects=True, vmem_limit_bytes=63 * 1024 * 1024
        ),
        cost_estimate=pl.CostEstimate(
            flops=2 * 2048 * 3072 * 256, bytes_accessed=2 * 1024 * 1024, transcendentals=0
        ),
    )(
        modes.reshape(3, M * CELLS, 128),
        metric.reshape(3 * CELLS, 128),
        block_map.reshape(CELLS, 128),
        flags.reshape(CELLS, 128),
        region_scale,
    )
    return summed.reshape(8, KS, 16).transpose(1, 2, 0)


def solution(mesh):
    return jax.shard_map(
        local,
        mesh=mesh,
        in_specs=(
            P(None, None, "grp", "blk", None),
            P(None, "grp", "blk", None),
            P("grp", "blk", None),
            P("grp", "blk", None),
            P(),
        ),
        out_specs=P(None, "grp", "blk"),
        check_vma=False,
    )
```
